256 devices in a mesh: pp: 8 (over x, core), ep: 32 (over z, y).
Axes of the slice: x: 4, y: 4, z: 8, core: 2. Of those that a mesh axis runs over, the one named last changes fastest.
Arguments:
- tokens: bfloat16 [4096, 7168], P('ep'), may hold values from -6 to 6
- expert_ids: int32 [4096, 4], P('ep'), may hold values from 0 to 31, all different within a row; in each aligned block of 128 rows (0 to 127, 128 to 255, ...) at most 24 rows name the same one
- route_score: float32 [4096, 4], P('ep'), may hold values from 0.05 to 1
- gate_weight: bfloat16 [32, 7168, 2048], P('ep', None, 'pp'), may hold values from -0.0625 to 0.0625
- up_weight: bfloat16 [32, 7168, 2048], P('ep', None, 'pp'), may hold values from -0.0625 to 0.0625
- down_weight: bfloat16 [32, 2048, 7168], P('ep', 'pp'), may hold values from -0.125 to 0.125
Outputs:
- layer_output: bfloat16 [4096, 7168], P('ep', 'pp')
The draws below stay inside these ranges and needn't reach their ends.
Inputs may be any that keep to these rules, and one draw needn't show every extreme that they name: `expert_ids`: each row names 4 different experts. Among the 128 tokens of one index of ep, no expert is named by more than 24 of them, a bound that some block reaches.
All inputs are finite; a program needn't handle non-finite values.
Results may differ from the reference program's by a relative error of at most 0.019.
Values may be sent and summed in bfloat16 or wider, within the bound.
A program may use at most 192 MiB of HBM per device.

```python
import math
import jax
import jax.numpy as jnp
import numpy as np
from jax import lax

D = 7168
FF = 2048
TOPK = 4
TOK_DEV = 128
EXPERTS = 32
CAP = 24
TOKENS = 4096
N_PP = 8
N_EP = 32


def steps_of(key, extent, cuts, least, top_value):
    level = 1.0
    for dim, shards_of in cuts:
        steps = jax.random.uniform(jax.random.fold_in(jax.random.fold_in(key, 6), dim), (shards_of,), jnp.float32, least / len(cuts), top_value / len(cuts))
        level = level * jnp.repeat(jnp.exp(steps), extent[dim] // shards_of).reshape((-1,) + (1,) * (len(extent) - 1 - dim))
    return level


def shared_out(stream_key, own, number, rows, count, top, limit, lean):
    sequence = jax.random.permutation(stream_key, count)
    packed, ordinary = portions_of(count, rows * top, limit, lean, True), portions_of(count, rows * top, limit, lean, False)
    places = jnp.arange(count)

    def named(sizes, turn):
        used = int((sizes > 0).sum())
        fixed = max(1, used // 4)
        moved = fixed + (places - fixed + turn * (used - fixed)) % max(1, count - fixed)
        return jnp.zeros((count,), jnp.int32).at[sequence[jnp.where(places < fixed, places, moved)]].set(jnp.asarray(sizes, jnp.int32))

    sizes = jnp.where(number % 4 == 0, named(packed, number // 4), named(ordinary, number - number // 4 - 1))
    mixed = jax.random.permutation(jax.random.fold_in(own, 3), count)
    donor, sink = mixed[0:count // 2 * 2:2], mixed[1:count // 2 * 2:2]
    room = jnp.minimum(sizes[donor] - 1, limit - sizes[sink]) // 2
    room = jnp.where((donor == sequence[0]) | (sink == sequence[0]) | (sizes[sink] == 0), 0, jnp.maximum(room, 0))
    moved = jax.random.randint(jax.random.fold_in(own, 4), (count // 2,), 0, 1 << 20) % (room + 1)
    sizes = sizes.at[donor].add(-moved).at[sink].add(moved)
    items = jnp.searchsorted(jnp.cumsum(sizes), jnp.arange(rows * top), side="right").astype(jnp.int32)
    grid = items.reshape(top, rows).T
    grid = grid[jax.random.permutation(jax.random.fold_in(own, 1), rows)]
    turn = jax.random.randint(jax.random.fold_in(own, 2), (rows, 1), 0, top)
    return jnp.take_along_axis(grid, (jnp.arange(top)[None, :] + turn) % top, axis=1)


def portions_of(count, total, bound, slope, full):
    portions = [(1 << 20) // math.isqrt(standing ** slope) + 1 for standing in range(1, count + 1)]
    largest = bound if full else min(bound, max(-(-total // count), total * portions[0] // sum(portions)))
    least = 1 if total - largest >= count - 1 else 0
    holding, surplus = [largest] + [least] * (count - 1), total - largest - least * (count - 1)
    while surplus > 0:
        movable = [i for i in range(1, count) if holding[i] < largest] or [i for i in range(1, count) if holding[i] < bound]
        mass, remaining = sum([portions[i] for i in movable]), surplus
        for i in movable:
            addition = min(bound - holding[i], max(1, remaining * portions[i] // mass), surplus)
            holding[i] = holding[i] + addition
            surplus = surplus - addition
    return np.array(holding)


def scatter_about(rng, dims, scale, limit, pieces=(), kind=jnp.bfloat16):
    values = scale * jax.random.normal(rng, dims, jnp.float32)
    if pieces:
        values = values * steps_of(rng, dims, pieces, -0.22, 0.18)
    return jnp.clip(values, -limit, limit).astype(kind)


def setup_inputs(seed: int = 0) -> dict:
    keys = jax.random.split(jax.random.key(seed), 7)
    tokens = scatter_about(keys[0], (TOKENS, D), 1.0, 6.0, ((0, 32),))
    expert_ids_keys = jax.random.split(jax.random.fold_in(keys[1], 1), TOKENS // TOK_DEV)
    expert_ids_turns = jax.random.permutation(jax.random.fold_in(keys[1], 3), TOKENS // TOK_DEV)
    expert_ids = jax.vmap(lambda own, number: shared_out(jax.random.fold_in(keys[1], 2), own, number, TOK_DEV, EXPERTS, TOPK, CAP, 1))(expert_ids_keys, expert_ids_turns).reshape((TOKENS, TOPK))
    route_score = jnp.clip(jnp.exp(math.log(1.0) - 2.9957323 * jax.random.uniform(keys[2], (TOKENS, TOPK), jnp.float32) ** steps_of(keys[2], (TOKENS, TOPK), ((0, 32),), -0.2, 0.2)), 0.05, 1.0)
    gate_weight = scatter_about(keys[3], (EXPERTS, D, FF), D ** -0.5, 0.0625, ((0, 32), (2, 8)))
    up_weight = scatter_about(keys[4], (EXPERTS, D, FF), D ** -0.5, 0.0625, ((0, 32), (2, 8)))
    down_weight = scatter_about(keys[5], (EXPERTS, FF, D), FF ** -0.5, 0.125, ((0, 32), (1, 8)))
    return dict(tokens=tokens, expert_ids=expert_ids, route_score=route_score, gate_weight=gate_weight, up_weight=up_weight, down_weight=down_weight)


def slot_target(block_ids, expert_count, capacity):
    flattened = block_ids.reshape(-1)
    one_hot = (flattened[:, None] == jnp.arange(expert_count, dtype=jnp.int32)[None, :]).astype(jnp.int32)
    earlier = jnp.cumsum(one_hot, axis=0, dtype=jnp.int32) - one_hot
    position = jnp.sum(earlier * one_hot, axis=1, dtype=jnp.int32)
    return (flattened * capacity + position).astype(jnp.int32)


def slot_owner(target, pair_count, buffer_size):
    owners = jnp.full((buffer_size,), pair_count, jnp.int32)
    return owners.at[target].set(jnp.arange(pair_count, dtype=jnp.int32))


def reference(tokens, expert_ids, route_score, gate_weight, up_weight, down_weight):
    route_weight = route_score / jnp.sum(route_score, axis=1, keepdims=True)
    pair_count = TOK_DEV * TOPK
    blocks = expert_ids.reshape(N_EP, TOK_DEV, TOPK)
    targets = jax.vmap(lambda block_ids: slot_target(block_ids, EXPERTS, CAP))(blocks)
    owners = jax.vmap(lambda target: slot_owner(target, pair_count, EXPERTS * CAP))(targets)
    filled = owners < pair_count
    safe_owner = jnp.where(filled, owners, 0).astype(jnp.int32)
    block_start = (jnp.arange(N_EP, dtype=jnp.int32) * TOK_DEV)[:, None]
    token_index = jnp.where(filled, safe_owner // TOPK + block_start, 0).astype(jnp.int32)
    pair_index = (safe_owner + jnp.arange(N_EP, dtype=jnp.int32)[:, None] * pair_count).astype(jnp.int32)
    slot_weight = jnp.where(filled, route_weight.reshape(-1)[pair_index], 0.0).astype(jnp.float32)

    def per_expert(values):
        return values.reshape(N_EP, EXPERTS, CAP).transpose(1, 0, 2).reshape(EXPERTS, N_EP * CAP)

    token_slots = per_expert(token_index)
    filled_slots = per_expert(filled)
    weight_slots = per_expert(slot_weight)
    share = FF // N_PP

    def expert_step(running, inputs):
        gate_one, up_one, down_one, token_rows, filled_rows, weight_rows = inputs
        expert_rows = jnp.where(filled_rows[:, None], tokens[token_rows], jnp.zeros((), jnp.bfloat16)).astype(jnp.bfloat16)
        gate_sum = jnp.dot(expert_rows, gate_one, preferred_element_type=jnp.float32)
        up_sum = jnp.dot(expert_rows, up_one, preferred_element_type=jnp.float32)
        hidden = (jax.nn.silu(gate_sum) * up_sum).astype(jnp.bfloat16)
        expert_output = jnp.zeros((N_EP * CAP, D), jnp.float32)
        for slice_index in range(N_PP):
            low = slice_index * share
            expert_part = jnp.dot(hidden[:, low:low + share], down_one[low:low + share], preferred_element_type=jnp.float32).astype(jnp.bfloat16)
            expert_output = expert_output + expert_part.astype(jnp.float32)
        running = running.at[token_rows].add(expert_output * weight_rows[:, None])
        return running, None

    start = jnp.zeros((TOKENS, D), jnp.float32)
    total, unused = lax.scan(expert_step, start, (gate_weight, up_weight, down_weight, token_slots, filled_slots, weight_slots))
    return total.astype(jnp.bfloat16)
```

```python
import jax
import jax.numpy as jnp
from jax import lax
from jax.experimental import pallas as pl
from jax.experimental.pallas import tpu as pltpu
from jax.sharding import PartitionSpec as P

MESH = pl.DeviceIdType.MESH
F32, BF16 = jnp.float32, jnp.bfloat16
D, REGION, CW = 7168, 1792, 256
TOK, CAP, NE, TOPK = 128, 24, 32, 4
NX, NZ, NY = 4, 8, 4
ROWS = NY * 4 * CAP
YR = 4 * CAP
HALF = ROWS // 2
NA, ND = 5, 8
NCH = NA + ND
NPIECE = 7


def kernel(meta_ref, tok, gate, up, down, out_ref, mine, metas, wgu, wd, T, GS, XA, acc, H, S, SWT, PX, RA, FX, Q, ZR, ZF, O,
           w_loc, w_send, w_recv, m_send, m_recv, z_send, z_recv, y_send, y_recv, x_send, x_recv,
           rx_send, rx_recv, ry_send, ry_recv, rz_send, rz_recv, o_send, o_recv):
    pp, ep = lax.axis_index("pp"), lax.axis_index("ep")
    x, c, z, y = lax.div(pp, 2), lax.rem(pp, 2), lax.div(ep, NY), lax.rem(ep, NY)
    sgn = 2 * c - 1

    def dev(dx=0, dz=0, dy=0):
        return (lax.rem(x + dx + NX, NX) * 2 + c, lax.rem(z + dz + NZ, NZ) * NY + lax.rem(y + dy, NY))

    def remote(src, dst, ss, rs, device):
        return pltpu.make_async_remote_copy(src_ref=src, dst_ref=dst, send_sem=ss, recv_sem=rs, device_id=device,
                                            device_id_type=MESH)

    sib = (x * 2 + 1 - c, ep)
    bar = pltpu.get_barrier_semaphore()
    for k in range(1, 8):
        pl.semaphore_signal(bar, inc=1, device_id=(lax.rem(pp + k, 8), ep), device_id_type=MESH)
        pl.semaphore_signal(bar, inc=1, device_id=dev(dz=k), device_id_type=MESH)
    for k in range(1, 4):
        pl.semaphore_signal(bar, inc=1, device_id=dev(dy=k), device_id_type=MESH)

    local = [
        pltpu.make_async_copy(gate, wgu.at[c], w_loc.at[0]),
        pltpu.make_async_copy(up, wgu.at[2 + c], w_loc.at[1]),
        pltpu.make_async_copy(down, wd.at[pl.ds(pl.multiple_of(c * 256, 256), 256)], w_loc.at[2]),
    ]
    for cp in local:
        cp.start()

    ids, score = meta_ref[0:4, :], meta_ref[4:8, :]
    e_iota = lax.broadcasted_iota(jnp.int32, (NE, TOK), 0).astype(F32)
    hot = [(e_iota == ids[k:k + 1, :]).astype(F32) for k in range(TOPK)]
    count = hot[0] + hot[1] + hot[2] + hot[3]
    before = (lax.broadcasted_iota(jnp.int32, (TOK, TOK), 0) < lax.broadcasted_iota(jnp.int32, (TOK, TOK), 1)).astype(F32)
    earlier = jnp.dot(count.astype(BF16), before.astype(BF16), preferred_element_type=F32)
    pos = [jnp.sum(h * earlier, axis=0, keepdims=True) for h in hot]
    mine[0:4, :] = ids * CAP + jnp.concatenate(pos, axis=0)
    mine[4:8, :] = score / jnp.sum(score, axis=0, keepdims=True)

    pl.semaphore_wait(bar, 17)

    def meta_copy(s):
        return remote(mine, metas.at[s], m_send.at[s], m_recv.at[s], dev(dz=sgn * (s + c)))

    @pl.when(c == 0)
    def _():
        metas[0] = mine[...]

    @pl.when(c == 1)
    def _():
        meta_copy(0).start()

    for s in range(1, 4):
        meta_copy(s).start()

    def col_a(r, j):
        return pl.multiple_of(REGION * r + CW * (j + lax.div(j, 3)), CW)

    def col_d(d):
        return pl.multiple_of(REGION * lax.div(d, 2) + CW * (3 + 3 * lax.rem(d, 2)), CW)

    def col(j):
        return pl.multiple_of(jnp.where(j < NA, col_a(x, j), col_d(j - NA)), CW)

    def slot(j):
        return jnp.where(j < NA, x * NA + j, 3 * NA + j)

    def stage(s):
        return pl.ds(s * TOK, TOK)

    def first_hop(j):
        return remote(tok.at[:, pl.ds(col(j), CW)], T.at[j, stage(0)], z_send.at[0, j], z_recv.at[0, j], dev(dz=sgn))

    def hop(s, j):
        return remote(T.at[j, stage(s - 1)], T.at[j, stage(s)], z_send.at[s, j], z_recv.at[s, j], dev(dz=sgn))

    def y_rows(k):
        return pl.ds(pl.multiple_of(k * YR, 32), YR)

    def y_copy(dy, j):
        there = lax.rem(y + dy, NY)
        return remote(GS.at[j, y_rows(there)], XA.at[slot(j), y_rows(y)], y_send.at[dy - 1, j], y_recv.at[dy - 1, j], dev(dy=dy))

    def x_copy(i, j):
        if i < 2:
            return remote(XA.at[x * NA + j], XA.at[x * NA + j], x_send.at[i, j], x_recv.at[i, j], dev(dx=1 - 2 * i))
        away = lax.rem(x + (3 if i == 2 else 1), NX) * NA + j
        part = pl.ds(0, HALF) if i == 2 else pl.ds(HALF, HALF)
        return remote(XA.at[away, part], XA.at[away, part], x_send.at[i, j], x_recv.at[i, j], dev(dx=1 if i == 2 else -1))

    def gate_up(sl, w_row):
        @pl.loop(0, 4)
        def _(i):
            acc[i] += jnp.dot(XA[sl], wgu[i, pl.ds(w_row, CW), :], preferred_element_type=F32)

    def within(j, n):
        return jnp.logical_and(j >= 0, j < n)

    w_copies = [
        remote(gate, wgu.at[c], w_send.at[0], w_recv.at[0], sib),
        remote(up, wgu.at[2 + c], w_send.at[1], w_recv.at[1], sib),
        remote(down, wd.at[pl.ds(pl.multiple_of(c * 256, 256), 256)], w_send.at[2], w_recv.at[2], sib),
    ]

    XS, XF, XM, LAG = 6, 8, 10, 6
    steps = max(NCH + LAG, XM + 2 * NA - 1)

    def dispatch(t, carry):
        @pl.when(t < NCH)
        def _():
            @pl.when(c == 0)
            def _():
                pltpu.make_async_copy(tok.at[:, pl.ds(col(t), CW)], T.at[t, stage(0)], z_recv.at[0, t]).start()

            @pl.when(c == 1)
            def _():
                first_hop(t).start()

        for h in range(3):
            j = t - 1 - h

            @pl.when(within(j, NCH))
            def _():
                first_hop(j).wait_recv() if h == 0 else hop(h, j).wait_recv()
                hop(h + 1, j).start()

        @pl.when(t == 0)
        def _():
            for cp in w_copies:
                cp.start()
            acc[...] = jnp.zeros_like(acc)

        @pl.when(t == 2)
        def _():
            @pl.when(c == 1)
            def _():
                meta_copy(0).wait()

            for s in range(1, 4):
                meta_copy(s).wait()
            p_iota = lax.broadcasted_iota(jnp.int32, (CAP, TOK), 0).astype(F32)
            empty = jnp.zeros((CAP, TOK), F32)
            for s in range(4):
                picks, weighted = [], []
                for yy in range(NY):
                    key = p_iota + ((z * NY + yy) * CAP).astype(F32)
                    eq = [(metas[s, k:k + 1, :] == key).astype(F32) for k in range(TOPK)]
                    pick = eq[0] + eq[1] + eq[2] + eq[3]
                    wpick = sum(eq[k] * metas[s, 4 + k:5 + k, :] for k in range(TOPK))
                    picks += [pick if s2 == s else empty for s2 in range(4)]
                    weighted += [wpick if s2 == s else empty for s2 in range(4)]
                S[:, s * TOK:(s + 1) * TOK] = jnp.concatenate(picks, axis=0).astype(BF16)
                SWT[s * TOK:(s + 1) * TOK, :] = jnp.concatenate(weighted, axis=0).T.astype(BF16)

        j_pick = t - 4

        @pl.when(within(j_pick, NCH))
        def _():
            hop(3, j_pick).wait_recv()
            GS[j_pick] = jnp.dot(S[...], T[j_pick], preferred_element_type=F32).astype(BF16)
            for dy in range(1, 4):
                y_copy(dy, j_pick).start()
            XA[slot(j_pick), y_rows(y), :] = GS[j_pick, y_rows(y), :]

        @pl.when(t == LAG)
        def _():
            for cp in local:
                cp.wait()
            for cp in w_copies[:2]:
                cp.wait()

        ja = t - XS

        @pl.when(jnp.logical_and(within(ja, 2 * NA), lax.rem(ja + 64, 2) == 0))
        def _():
            j = lax.div(ja, 2)
            for dy in range(1, 4):
                y_copy(dy, j).wait()
            x_copy(0, j).start()
            x_copy(1, j).start()

        jf = t - XF

        @pl.when(jnp.logical_and(within(jf, 2 * NA), lax.rem(jf + 64, 2) == 0))
        def _():
            j = lax.div(jf, 2)
            x_copy(0, j).wait()
            x_copy(2, j).start()
            x_copy(1, j).wait()
            x_copy(3, j).start()

        jd = t - LAG

        @pl.when(jnp.logical_and(jd >= NA, jd < NCH))
        def _():
            for dy in range(1, 4):
                y_copy(dy, jd).wait()
            gate_up(3 * NA + jd, col_d(jd - NA))

        jm = t - XM

        @pl.when(jnp.logical_and(within(jm, 2 * NA), lax.rem(jm + 64, 2) == 0))
        def _():
            j = lax.div(jm, 2)
            x_copy(2, j).wait()
            x_copy(3, j).wait()

            @pl.loop(0, NX)
            def _(r):
                gate_up(r * NA + j, col_a(r, j))

        for h in range(4):
            j = t - 2 - h

            @pl.when(within(j, NCH))
            def _():
                if h == 0:
                    pl.when(c == 1)(lambda: first_hop(j).wait_send())
                else:
                    hop(h, j).wait_send()

        return carry

    lax.fori_loop(0, steps, dispatch, 0)

    for i in range(2):
        g = acc[i]
        H[:, i * 256:(i + 1) * 256] = (g / (1.0 + jnp.exp(-g)) * acc[2 + i]).astype(BF16)
    w_copies[2].wait()

    right, left, anti = lax.rem(x + 1, NX), lax.rem(x + 3, NX), lax.rem(x + 2, NX)
    lo, hi = pl.ds(0, HALF), pl.ds(HALF, HALF)

    def rx_copy(i, j):
        src, dst, dx = [
            (PX.at[j, anti, lo], RA.at[0, j], 1),
            (PX.at[j, anti, hi], RA.at[1, j], -1),
            (PX.at[j, right, hi], FX.at[0, j, hi], 1),
            (PX.at[j, left, lo], FX.at[1, j, lo], -1),
            (PX.at[j, right, lo], FX.at[0, j, lo], 1),
            (PX.at[j, left, hi], FX.at[1, j, hi], -1),
        ][i]
        return remote(src, dst, rx_send.at[i, j], rx_recv.at[i, j], dev(dx=dx))

    def ry_copy(dy, j):
        there = lax.rem(y + dy, NY)
        return remote(GS.at[j, y_rows(there)], Q.at[j, y_rows(y)], ry_send.at[dy - 1, j], ry_recv.at[dy - 1, j], dev(dy=dy))

    def rz_copy(s, j):
        if s == 0:
            return remote(T.at[j, stage(0)], ZF.at[j], rz_send.at[0, j], rz_recv.at[0, j], dev(dz=-sgn))
        return remote(T.at[j, stage(s)], ZR.at[j, stage(s - 1)], rz_send.at[s, j], rz_recv.at[s, j], dev(dz=-sgn))

    def local_chunk(q):
        return jnp.where(q < ND, NA + q, q - ND)

    def out_copy(h, j):
        d = j - NA
        region = jnp.where(j < NA, x, lax.div(jnp.maximum(d, 0), 2))
        i = jnp.where(j < NA, j + lax.div(j, 3), 3 + 3 * lax.rem(jnp.maximum(d, 0), 2))
        p = 2 * i + h
        owner = lax.div(p, NPIECE)
        place = lax.rem(p, NPIECE)
        there = region * 2 + owner
        return there, place, remote(ZF.at[j, :, pl.ds(h * 128, 128)], O.at[place, pp], o_send.at[h, j], o_recv.at[place, pp],
                                    (there, ep))

    def back(t, carry):
        @pl.when(jnp.logical_and(t < 2 * NA, lax.rem(t, 2) == 0))
        def _():
            j = lax.div(t, 2)

            @pl.loop(0, NX)
            def _(r):
                PX[j, r] = jnp.dot(H[...], wd[:, pl.ds(col_a(r, j), CW)], preferred_element_type=F32).astype(BF16)

            for i in range(4):
                rx_copy(i, j).start()

        @pl.when(jnp.logical_and(within(t - 2, 2 * NA), lax.rem(t, 2) == 0))
        def _():
            j = lax.div(t - 2, 2)
            rx_copy(0, j).wait()
            PX[j, right, lo, :] = (PX[j, right, lo, :].astype(F32) + RA[0, j].astype(F32)).astype(BF16)
            rx_copy(4, j).start()
            rx_copy(1, j).wait()
            PX[j, left, hi, :] = (PX[j, left, hi, :].astype(F32) + RA[1, j].astype(F32)).astype(BF16)
            rx_copy(5, j).start()

        @pl.when(jnp.logical_and(within(t - 4, 2 * NA), lax.rem(t, 2) == 0))
        def _():
            j = lax.div(t - 4, 2)
            for i in range(2, 6):
                rx_copy(i, j).wait()
            GS[j] = (PX[j, x].astype(F32) + FX[0, j].astype(F32) + FX[1, j].astype(F32)).astype(BF16)

        @pl.when(t < NCH)
        def _():
            j = local_chunk(t)

            @pl.when(t < ND)
            def _():
                GS[j] = jnp.dot(H[...], wd[:, pl.ds(col_d(t), CW)], preferred_element_type=F32).astype(BF16)

            for dy in range(1, 4):
                ry_copy(dy, j).start()
            Q[j, y_rows(y), :] = GS[j, y_rows(y), :]

        @pl.when(within(t - 2, NCH))
        def _():
            j = local_chunk(t - 2)
            for dy in range(1, 4):
                ry_copy(dy, j).wait()
            T[j] = jnp.dot(SWT[...], Q[j], preferred_element_type=F32).astype(BF16)
            rz_copy(3, j).start()

        for s in (2, 1, 0):
            @pl.when(within(t - 5 + s, NCH))
            def _():
                j = local_chunk(t - 5 + s)
                rz_copy(s + 1, j).wait()
                total = (T[j, stage(s), :].astype(F32) + ZR[j, stage(s), :].astype(F32)).astype(BF16)
                if s > 0:
                    T[j, stage(s), :] = total
                    rz_copy(s, j).start()
                else:
                    @pl.when(c == 0)
                    def _():
                        ZF[j] = total

                    @pl.when(c == 1)
                    def _():
                        T[j, stage(0), :] = total
                        rz_copy(0, j).start()

        @pl.when(within(t - 6, NCH))
        def _():
            j = local_chunk(t - 6)

            @pl.when(c == 1)
            def _():
                rz_copy(0, j).wait()

            for h in range(2):
                there, place, cp = out_copy(h, j)

                @pl.when(there != pp)
                def _():
                    cp.start()

                @pl.when(there == pp)
                def _():
                    O[place, pp] = ZF[j, :, h * 128:(h + 1) * 128]

        return carry

    lax.fori_loop(0, NCH + 6, back, 0)

    def sent(j, carry):
        for h in range(2):
            there, place, cp = out_copy(h, j)

            @pl.when(there != pp)
            def _():
                cp.wait_send()
        return carry

    lax.fori_loop(0, NCH, sent, 0)

    for place in range(NPIECE):
        p = c * NPIECE + place
        i = lax.div(p, 2)
        summed = lax.rem(i, 3) == 0

        def arrived(src):
            remote(O.at[place, src], O.at[place, src], o_send.at[0, 0], o_recv.at[place, src], sib).wait_recv()

        is_d = jnp.logical_and(i > 0, summed)

        @pl.when(is_d)
        def _():
            for k in range(1, 8):
                arrived(lax.rem(pp + k, 8))
            total = O[place, 0].astype(F32)
            for k in range(1, 8):
                total += O[place, k].astype(F32)
            out_ref[:, place * 128:(place + 1) * 128] = total.astype(BF16)

        @pl.when(jnp.logical_not(is_d))
        def _():
            arrived(x * 2 + 1 - c)
            out_ref[:, place * 128:(place + 1) * 128] = (O[place, x * 2].astype(F32) + O[place, x * 2 + 1].astype(F32)).astype(BF16)


def per_device(tokens, expert_ids, route_score, gate_weight, up_weight, down_weight):
    meta = jnp.concatenate([expert_ids.astype(F32), route_score], axis=1).T
    vm, dma = pltpu.VMEM, pltpu.SemaphoreType.DMA
    hbm = pl.BlockSpec(memory_space=pl.ANY)
    return pl.pallas_call(
        kernel,
        out_shape=jax.ShapeDtypeStruct((TOK, NPIECE * 128), BF16),
        in_specs=[pl.BlockSpec(memory_space=vm), hbm, hbm, hbm, hbm],
        out_specs=pl.BlockSpec(memory_space=vm),
        scratch_shapes=[
            vm((8, TOK), F32), vm((4, 8, TOK), F32),
            vm((4, D, 256), BF16), vm((512, D), BF16),
            vm((NCH, 4 * TOK, CW), BF16),
            vm((NCH, ROWS, CW), BF16),
            vm((4 * NA + ND, ROWS, CW), BF16),
            vm((4, ROWS, 256), F32), vm((ROWS, 512), BF16),
            vm((ROWS, 4 * TOK), BF16), vm((4 * TOK, ROWS), BF16),
            vm((NA, NX, ROWS, CW), BF16),
            vm((2, NA, HALF, CW), BF16), vm((2, NA, ROWS, CW), BF16),
            vm((NCH, ROWS, CW), BF16),
            vm((NCH, 3 * TOK, CW), BF16), vm((NCH, TOK, CW), BF16),
            vm((NPIECE, 8, TOK, 128), BF16),
            dma((3,)), dma((3,)), dma((3,)), dma((4,)), dma((4,)),
            dma((4, NCH)), dma((4, NCH)), dma((3, NCH)), dma((3, NCH)), dma((4, NA)), dma((4, NA)),
            dma((6, NA)), dma((6, NA)), dma((3, NCH)), dma((3, NCH)), dma((4, NCH)), dma((4, NCH)),
            dma((2, NCH)), dma((NPIECE, 8)),
        ],
        compiler_params=pltpu.CompilerParams(collective_id=0, has_side_effects=True, vmem_limit_bytes=62 * 2**20),
        name="moe",
    )(meta, tokens, gate_weight[0], up_weight[0], down_weight[0])


def solution(mesh):
    placed = (
        P("ep", None),
        P("ep", None),
        P("ep", None),
        P("ep", None, "pp"),
        P("ep", None, "pp"),
        P("ep", "pp", None),
    )
    return jax.shard_map(
        per_device, mesh=mesh, in_specs=placed, out_specs=P("ep", "pp"), check_vma=False
    )
```

```python
import jax
import jax.numpy as jnp
from jax import lax
from jax.experimental import pallas as pl
from jax.experimental.pallas import tpu as pltpu
from jax.sharding import PartitionSpec as P

MESH = pl.DeviceIdType.MESH
F32, BF16 = jnp.float32, jnp.bfloat16
D, REGION, CW, HW = 7168, 1792, 256, 128
TOK, CAP, NE, TOPK = 128, 24, 32, 4
NX, NZ, NY = 4, 8, 4
NB = 8
BR = 2 * CAP
SENT = NB * BR
ROWS = NB * CAP
HALF = ROWS // 2
NJ = REGION // CW
NU = 2 * NJ
NPIECE = 7
LX, LF, LM = 1, 3, 5
LP = NJ + LM
LA, LS, LC, LO = LP + 2, LP + 4, LP + 6, LP + 7


def kernel(ids_ref, score_ref, tok, gate, up, down, out_ref, wgu, wd, tokv, GS, PK, XA, acc, H, S, WW, PX, RA, FX, GB, Q, ZF, ZO, O,
           l_sem, w_send, w_recv, a_send, a_recv, x_send, x_recv, rx_send, rx_recv, b_send, b_recv, o_send, o_recv):
    pp, ep = lax.axis_index("pp"), lax.axis_index("ep")
    x, c, z, y = lax.div(pp, 2), lax.rem(pp, 2), lax.div(ep, NY), lax.rem(ep, NY)
    sgn = 2 * c - 1

    def dev(dx=0, dz=0, dy=0):
        return (lax.rem(x + dx + NX, NX) * 2 + c, lax.rem(z + dz + NZ, NZ) * NY + lax.rem(y + dy, NY))

    def remote(src, dst, ss, rs, device):
        return pltpu.make_async_remote_copy(src_ref=src, dst_ref=dst, send_sem=ss, recv_sem=rs, device_id=device,
                                            device_id_type=MESH)

    sib = (x * 2 + 1 - c, ep)
    bar = pltpu.get_barrier_semaphore()

    def greet(device):
        pl.semaphore_signal(bar, inc=1, device_id=device, device_id_type=MESH)

    for dx in (1, 2, 3):
        greet(dev(dx=dx))
    greet(sib)
    for dy in range(NY):
        for dz in (1, 2, 3, 5, 6, 7):
            greet(dev(dz=dz, dy=dy))

    @pl.when(c == 0)
    def _():
        for dy in range(1, NY):
            greet(dev(dy=dy))

    @pl.when(c == 1)
    def _():
        for dy in range(NY):
            greet(dev(dz=4, dy=dy))

    own_rows = pl.ds(pl.multiple_of(c * 256, 256), 256)
    tok_copy = pltpu.make_async_copy(tok, tokv, l_sem.at[3])
    local = [
        pltpu.make_async_copy(gate, wgu.at[c], l_sem.at[0]),
        pltpu.make_async_copy(up, wgu.at[2 + c], l_sem.at[1]),
        pltpu.make_async_copy(down, wd.at[own_rows], l_sem.at[2]),
    ]
    for cp in [tok_copy] + local:
        cp.start()

    ids, score = ids_ref[...].astype(F32), score_ref[...]
    e_iota = lax.broadcasted_iota(jnp.int32, (NE, TOK), 0).astype(F32)
    hot = [(e_iota == ids[k:k + 1, :]).astype(F32) for k in range(TOPK)]
    count = hot[0] + hot[1] + hot[2] + hot[3]
    before = (lax.broadcasted_iota(jnp.int32, (TOK, TOK), 0) < lax.broadcasted_iota(jnp.int32, (TOK, TOK), 1)).astype(F32)
    earlier = jnp.dot(count.astype(BF16), before.astype(BF16), preferred_element_type=F32)
    target = ids * CAP + jnp.concatenate([jnp.sum(h * earlier, axis=0, keepdims=True) for h in hot], axis=0)
    weight = score / jnp.sum(score, axis=0, keepdims=True)

    p_iota = lax.broadcasted_iota(jnp.int32, (CAP, TOK), 0).astype(F32)
    empty = jnp.zeros((CAP, TOK), F32)

    def slot_matches(g, k):
        expert = lax.rem(z + sgn * ((g if k % 2 == 0 else 3 - g) + c) + NZ, NZ) * NY + k // 2
        key = p_iota + (expert * CAP).astype(F32)
        return [(target[i:i + 1, :] == key).astype(F32) for i in range(TOPK)]

    def halves(a):
        return jnp.concatenate([jnp.concatenate([a, empty], axis=1), jnp.concatenate([empty, a], axis=1)], axis=0)

    def pick_slots(g):
        for k in range(NB):
            eq = slot_matches(g, k)
            at = g * SENT + k * BR
            S[at:at + BR, :] = halves(eq[0] + eq[1] + eq[2] + eq[3]).astype(BF16)

    def weigh_slots(g):
        rows = []
        for k in range(NB):
            eq = slot_matches(g, k)
            rows.append(halves(sum(eq[i] * weight[i:i + 1, :] for i in range(TOPK))))
        WW[:, g * SENT:(g + 1) * SENT] = jnp.concatenate(rows, axis=0).T.astype(BF16)

    pick_slots(0)

    def parts(u):
        return lax.div(u, NJ), lax.rem(u, NJ)

    def col(r, j):
        return pl.multiple_of(REGION * r + CW * j, CW)

    def block(k):
        return pl.ds(pl.multiple_of(k * BR, 16), BR)

    def scatter(src, dst, ss, rs, u, way):
        g = lax.div(u, NJ)
        whole = jnp.logical_or(c == 1, g == 1)
        for s2 in (1, 0):
            dz = way * sgn * ((3 - g if s2 else g) + c)
            for dy in range(NY):
                cp = remote(src.at[u, block(lax.rem(y + dy, NY) * 2 + s2)], dst.at[u, block(y * 2 + s2)], ss.at[u], rs.at[u],
                            dev(dz=dz, dy=dy))
                if s2 or dy:
                    cp.start()
                else:
                    pl.when(whole)(cp.start)

        @pl.when(jnp.logical_not(whole))
        def _():
            pltpu.make_async_copy(src.at[u, block(y * 2)], dst.at[u, block(y * 2)], rs.at[u]).start()

    def all_arrived(dst, rs, u):
        remote(dst.at[u], dst.at[u], rs.at[u], rs.at[u], sib).wait_recv()

    def all_left(src, ss, u):
        whole = jnp.logical_or(c == 1, lax.div(u, NJ) == 1)

        @pl.when(whole)
        def _():
            remote(src.at[u], src.at[u], ss.at[u], ss.at[u], sib).wait_send()

        @pl.when(jnp.logical_not(whole))
        def _():
            most = src.at[u, pl.ds(0, SENT - BR)]
            remote(most, most, ss.at[u], ss.at[u], sib).wait_send()

    def x_copy(i, u):
        if i < 2:
            return remote(XA.at[x, u], XA.at[x, u], x_send.at[i, u], x_recv.at[i, u], dev(dx=1 - 2 * i))
        away = lax.rem(x + (3 if i == 2 else 1), NX)
        part = pl.ds(0, HALF) if i == 2 else pl.ds(HALF, HALF)
        return remote(XA.at[away, u, part], XA.at[away, u, part], x_send.at[i, u], x_recv.at[i, u], dev(dx=1 if i == 2 else -1))

    right, left, anti = lax.rem(x + 1, NX), lax.rem(x + 3, NX), lax.rem(x + 2, NX)
    lo, hi = pl.ds(0, HALF), pl.ds(HALF, HALF)

    def rx_copy(i, u):
        src, dst, dx = [
            (PX.at[u, anti, lo], RA.at[0, u], 1),
            (PX.at[u, anti, hi], RA.at[1, u], -1),
            (PX.at[u, right, hi], FX.at[0, u, hi], 1),
            (PX.at[u, left, lo], FX.at[1, u, lo], -1),
            (PX.at[u, right, lo], FX.at[0, u, lo], 1),
            (PX.at[u, left, hi], FX.at[1, u, hi], -1),
        ][i]
        return remote(src, dst, rx_send.at[i, u], rx_recv.at[i, u], dev(dx=dx))

    def piece(h, j):
        return lax.div(2 * j + h, NPIECE), lax.rem(2 * j + h, NPIECE)

    def out_copy(h, j):
        place = piece(h, j)[1]
        return remote(ZO.at[j, pl.ds(h * TOK, TOK)], O.at[place], o_send.at[h, j], o_recv.at[place], sib)

    w_copies = [
        remote(gate, wgu.at[c], w_send.at[0], w_recv.at[0], sib),
        remote(up, wgu.at[2 + c], w_send.at[1], w_recv.at[1], sib),
        remote(down, wd.at[own_rows], w_send.at[2], w_recv.at[2], sib),
    ]

    def send_rows(u):
        g, j = parts(u)
        at = col(x, j)
        both = jnp.concatenate([tokv[:, pl.ds(at, HW)], tokv[:, pl.ds(pl.multiple_of(at + HW, HW), HW)]], axis=0)
        rows = pl.ds(pl.multiple_of(g * SENT, SENT), SENT)
        GS[u] = jnp.dot(S[rows, :], both, preferred_element_type=F32).astype(BF16)
        scatter(GS, PK, a_send, a_recv, u, 1)

    @pl.when(c == 0)
    def _():
        pl.semaphore_wait(bar, 4 + 27)

    @pl.when(c == 1)
    def _():
        pl.semaphore_wait(bar, 4 + 28)

    tok_copy.wait()
    send_rows(0)

    def step(t, carry):
        def unit(lag, f):
            u = t - lag

            @pl.when(jnp.logical_and(u >= 0, u < NU))
            def _():
                f(u)

        @pl.when(t < NU - 1)
        def _():
            send_rows(t + 1)

        @pl.when(t == 0)
        def _():
            for cp in w_copies:
                cp.start()
            acc[...] = jnp.zeros_like(acc)
            pick_slots(1)

        def forward(u):
            x_copy(0, u).wait()
            x_copy(2, u).start()
            x_copy(1, u).wait()
            x_copy(3, u).start()

        unit(LF, forward)

        def send_x(u):
            all_arrived(PK, a_recv, u)
            a = PK[u].astype(F32).reshape(NB, BR, HW)
            XA[x, u] = jnp.concatenate([a[:, :CAP].reshape(ROWS, HW), a[:, CAP:].reshape(ROWS, HW)], axis=1).astype(BF16)
            x_copy(0, u).start()
            x_copy(1, u).start()

        unit(LX, send_x)

        def add_x(u):
            rx_copy(0, u).wait()
            PX[u, right, lo, :] = (PX[u, right, lo, :].astype(F32) + RA[0, u].astype(F32)).astype(BF16)
            rx_copy(4, u).start()
            rx_copy(1, u).wait()
            PX[u, left, hi, :] = (PX[u, left, hi, :].astype(F32) + RA[1, u].astype(F32)).astype(BF16)
            rx_copy(5, u).start()

        unit(LA, add_x)

        @pl.when(jnp.logical_or(t == LP, t == LP + NJ))
        def _():
            g = lax.div(t - LP, NJ)
            for i in range(2):
                v = acc[g, i]
                H[g, :, i * 256:(i + 1) * 256] = (v / (1.0 + jnp.exp(-v)) * acc[g, 2 + i]).astype(BF16)

        @pl.when(t == LP)
        def _():
            local[2].wait()
            w_copies[2].wait()

        def down_part(u):
            g, j = parts(u)

            @pl.loop(0, NX)
            def _(i):
                r = lax.rem(x + 2 + i, NX)
                PX[u, r] = jnp.dot(H[g], wd[:, pl.ds(col(r, j), CW)], preferred_element_type=F32).astype(BF16)

            for i in range(4):
                rx_copy(i, u).start()

        unit(LP, down_part)

        def sum_x(u):
            for i in range(2, 6):
                rx_copy(i, u).wait()
            a = PX[u, x].astype(F32) + FX[0, u].astype(F32) + FX[1, u].astype(F32)
            a = jnp.concatenate([a[:, :HW].reshape(NB, CAP, HW), a[:, HW:].reshape(NB, CAP, HW)], axis=1)
            GB[u] = a.reshape(SENT, HW).astype(BF16)
            scatter(GB, Q, b_send, b_recv, u, -1)

        unit(LS, sum_x)

        @pl.when(t == 1)
        def _():
            weigh_slots(0)

        @pl.when(t == 2)
        def _():
            weigh_slots(1)

        @pl.when(t == LM)
        def _():
            for cp in local[:2] + w_copies[:2]:
                cp.wait()

        def gate_up(u):
            g, j = parts(u)
            x_copy(2, u).wait()
            x_copy(3, u).wait()

            @pl.loop(0, 4)
            def _(i):
                acc[g, i] += sum(jnp.dot(XA[r, u], wgu[i, pl.ds(col(r, j), CW), :], preferred_element_type=F32)
                                 for r in range(NX))

        unit(LM, gate_up)

        def combine(u):
            g, j = parts(u)
            all_arrived(Q, b_recv, u)
            cols = pl.ds(pl.multiple_of(g * SENT, SENT), SENT)
            part = jnp.dot(WW[:, cols], Q[u], preferred_element_type=F32)

            @pl.when(g == 0)
            def _():
                ZF[j] = part

            @pl.when(g == 1)
            def _():
                ZF[j] += part
                for h in range(2):
                    @pl.when(piece(h, j)[0] != c)
                    def _():
                        ZO[j, h * TOK:(h + 1) * TOK, :] = ZF[j, h * TOK:(h + 1) * TOK, :].astype(BF16)
                        out_copy(h, j).start()

        unit(LC, combine)

        def finish(u):
            j = u - NJ

            @pl.when(j >= 0)
            def _():
                for h in range(2):
                    core, place = piece(h, j)

                    @pl.when(core == c)
                    def _():
                        out_copy(h, j).wait_recv()
                        at = pl.ds(pl.multiple_of(place * HW, HW), HW)
                        out_ref[:, at] = (ZF[j, h * TOK:(h + 1) * TOK, :] + O[place].astype(F32)).astype(BF16)

                    @pl.when(core != c)
                    def _():
                        out_copy(h, j).wait_send()

        unit(LO, finish)
        unit(LX + 2, lambda u: all_left(GS, a_send, u))
        unit(LO, lambda u: all_left(GB, b_send, u))
        return carry

    lax.fori_loop(0, NU + LO, step, 0)


def per_device(tokens, expert_ids, route_score, gate_weight, up_weight, down_weight):
    vm, dma = pltpu.VMEM, pltpu.SemaphoreType.DMA
    hbm, here = pl.BlockSpec(memory_space=pl.ANY), pl.BlockSpec(memory_space=pltpu.VMEM)
    return pl.pallas_call(
        kernel,
        out_shape=jax.ShapeDtypeStruct((TOK, NPIECE * HW), BF16),
        in_specs=[here, here, hbm, hbm, hbm, hbm],
        out_specs=here,
        scratch_shapes=[
            vm((4, D, 256), BF16), vm((512, D), BF16), vm((TOK, D), BF16),
            vm((NU, SENT, HW), BF16), vm((NU, SENT, HW), BF16),
            vm((NX, NU, ROWS, CW), BF16),
            vm((2, 4, ROWS, 256), F32), vm((2, ROWS, 512), BF16),
            vm((2 * SENT, 2 * TOK), BF16), vm((2 * TOK, 2 * SENT), BF16),
            vm((NU, NX, ROWS, CW), BF16),
            vm((2, NU, HALF, CW), BF16), vm((2, NU, ROWS, CW), BF16),
            vm((NU, SENT, HW), BF16), vm((NU, SENT, HW), BF16),
            vm((NJ, 2 * TOK, HW), F32), vm((NJ, 2 * TOK, HW), BF16),
            vm((NPIECE, TOK, HW), BF16),
            dma((4,)), dma((3,)), dma((3,)), dma((NU,)), dma((NU,)), dma((4, NU)), dma((4, NU)),
            dma((6, NU)), dma((6, NU)), dma((NU,)), dma((NU,)), dma((2, NJ)), dma((NPIECE,)),
        ],
        compiler_params=pltpu.CompilerParams(collective_id=0, has_side_effects=True, vmem_limit_bytes=62 * 2**20),
        name="moe",
    )(expert_ids.T, route_score.T, tokens, gate_weight[0], up_weight[0], down_weight[0])


def solution(mesh):
    placed = (
        P("ep", None),
        P("ep", None),
        P("ep", None),
        P("ep", None, "pp"),
        P("ep", None, "pp"),
        P("ep", "pp", None),
    )
    return jax.shard_map(
        per_device, mesh=mesh, in_specs=placed, out_specs=P("ep", "pp"), check_vma=False
    )
```

```python
import jax
import jax.numpy as jnp
from jax import lax
from jax.experimental import pallas as pl
from jax.experimental.pallas import tpu as pltpu
from jax.sharding import PartitionSpec as P

MESH = pl.DeviceIdType.MESH
F32, BF16 = jnp.float32, jnp.bfloat16
D, REGION, CW, HW = 7168, 1792, 256, 128
TOK, CAP, NE, TOPK = 128, 24, 32, 4
NX, NZ, NY = 4, 8, 4
NB = 8
BR = 2 * CAP
SENT = NB * BR
ROWS = NB * CAP
HALF = ROWS // 2
NJ = REGION // CW
NU = 2 * NJ
NK, NA = 6, 6
NRA = NA - NK
NR = NRA + NX * (NJ - NA)
YR = 2 * CAP
PLACE = (0, 2, 3, 1)
NPIECE = 7
LX, LF, LM = 1, 3, 5
LP = NJ + LM
LA, LS, LC, LO = LP + 2, LP + 4, LP + 6, LP + 7
LD = 2
RING = ((0, -1, 0), (1, -1, 2), (2, -1, 4), (3, -1, 6))


def kernel(ids_ref, score_ref, tok, gate, up, down, out_ref, wgu, wd, tokv, GS, PK, XA, acc, H, S, WW, PX, RA, FX, GB, Q, ZF, ZO, O,
           mine, metas, T, SR, GR,
           l_sem, w_send, w_recv, a_send, a_recv, x_send, x_recv, rx_send, rx_recv, b_send, b_recv, o_send, o_recv,
           m_send, m_recv, z_send, z_recv, y_send, y_recv):
    pp, ep = lax.axis_index("pp"), lax.axis_index("ep")
    x, c, z, y = lax.div(pp, 2), lax.rem(pp, 2), lax.div(ep, NY), lax.rem(ep, NY)
    sgn = 2 * c - 1

    def dev(dx=0, dz=0, dy=0):
        return (lax.rem(x + dx + NX, NX) * 2 + c, lax.rem(z + dz + NZ, NZ) * NY + lax.rem(y + dy, NY))

    def remote(src, dst, ss, rs, device):
        return pltpu.make_async_remote_copy(src_ref=src, dst_ref=dst, send_sem=ss, recv_sem=rs, device_id=device,
                                            device_id_type=MESH)

    sib = (x * 2 + 1 - c, ep)
    bar = pltpu.get_barrier_semaphore()

    def greet(device):
        pl.semaphore_signal(bar, inc=1, device_id=device, device_id_type=MESH)

    for dx in (1, 2, 3):
        greet(dev(dx=dx))
    greet(sib)
    for dy in range(NY):
        for dz in (1, 2, 3, 5, 6, 7):
            greet(dev(dz=dz, dy=dy))

    @pl.when(c == 0)
    def _():
        for dy in range(1, NY):
            greet(dev(dy=dy))

    @pl.when(c == 1)
    def _():
        for dy in range(NY):
            greet(dev(dz=4, dy=dy))

    own_rows = pl.ds(pl.multiple_of(c * 256, 256), 256)
    tok_copy = pltpu.make_async_copy(tok, tokv, l_sem.at[3])
    local = [
        pltpu.make_async_copy(gate, wgu.at[c], l_sem.at[0]),
        pltpu.make_async_copy(up, wgu.at[2 + c], l_sem.at[1]),
        pltpu.make_async_copy(down, wd.at[own_rows], l_sem.at[2]),
    ]
    for cp in [tok_copy] + local:
        cp.start()

    ids, score = ids_ref[...].astype(F32), score_ref[...]
    e_iota = lax.broadcasted_iota(jnp.int32, (NE, TOK), 0).astype(F32)
    hot = [(e_iota == ids[k:k + 1, :]).astype(F32) for k in range(TOPK)]
    count = hot[0] + hot[1] + hot[2] + hot[3]
    before = (lax.broadcasted_iota(jnp.int32, (TOK, TOK), 0) < lax.broadcasted_iota(jnp.int32, (TOK, TOK), 1)).astype(F32)
    earlier = jnp.dot(count.astype(BF16), before.astype(BF16), preferred_element_type=F32)
    target = ids * CAP + jnp.concatenate([jnp.sum(h * earlier, axis=0, keepdims=True) for h in hot], axis=0)
    weight = score / jnp.sum(score, axis=0, keepdims=True)

    p_iota = lax.broadcasted_iota(jnp.int32, (CAP, TOK), 0).astype(F32)
    empty = jnp.zeros((CAP, TOK), F32)

    def slot_matches(g, k):
        expert = lax.rem(z + sgn * ((g if k % 2 == 0 else 3 - g) + c) + NZ, NZ) * NY + k // 2
        key = p_iota + (expert * CAP).astype(F32)
        return [(target[i:i + 1, :] == key).astype(F32) for i in range(TOPK)]

    def halves(a):
        return jnp.concatenate([jnp.concatenate([a, empty], axis=1), jnp.concatenate([empty, a], axis=1)], axis=0)

    def pick_slots(g):
        for k in range(NB):
            eq = slot_matches(g, k)
            at = g * SENT + k * BR
            S[at:at + BR, :] = halves(eq[0] + eq[1] + eq[2] + eq[3]).astype(BF16)

    def weigh_slots(g):
        rows = []
        for k in range(NB):
            eq = slot_matches(g, k)
            rows.append(halves(sum(eq[i] * weight[i:i + 1, :] for i in range(TOPK))))
        WW[:, g * SENT:(g + 1) * SENT] = jnp.concatenate(rows, axis=0).T.astype(BF16)

    pick_slots(0)
    mine[0:4, :] = target
    mine[4:8, :] = weight

    def parts(u):
        return lax.div(u, NJ), lax.rem(u, NJ)

    def col(r, j):
        return pl.multiple_of(REGION * r + CW * j, CW)

    def block(k):
        return pl.ds(pl.multiple_of(k * BR, 16), BR)

    def scatter(src, dst, ss, rs, u, way):
        g = lax.div(u, NJ)
        whole = jnp.logical_or(c == 1, g == 1)
        for s2 in (1, 0):
            dz = way * sgn * ((3 - g if s2 else g) + c)
            for dy in range(NY):
                cp = remote(src.at[u, block(lax.rem(y + dy, NY) * 2 + s2)], dst.at[u, block(y * 2 + s2)], ss.at[u], rs.at[u],
                            dev(dz=dz, dy=dy))
                if s2 or dy:
                    cp.start()
                else:
                    pl.when(whole)(cp.start)

        @pl.when(jnp.logical_not(whole))
        def _():
            pltpu.make_async_copy(src.at[u, block(y * 2)], dst.at[u, block(y * 2)], rs.at[u]).start()

    def all_arrived(dst, rs, u):
        remote(dst.at[u], dst.at[u], rs.at[u], rs.at[u], sib).wait_recv()

    def all_left(src, ss, u):
        whole = jnp.logical_or(c == 1, lax.div(u, NJ) == 1)

        @pl.when(whole)
        def _():
            remote(src.at[u], src.at[u], ss.at[u], ss.at[u], sib).wait_send()

        @pl.when(jnp.logical_not(whole))
        def _():
            most = src.at[u, pl.ds(0, SENT - BR)]
            remote(most, most, ss.at[u], ss.at[u], sib).wait_send()

    def stage(s):
        return pl.ds(PLACE[s] * TOK, TOK)

    def hop(s, n, at):
        src = tokv.at[:, pl.ds(at, CW)] if s == 0 else T.at[n, stage(s - 1)]
        return remote(src, T.at[n, stage(s)], z_send.at[s, n], z_recv.at[s, n], dev(dz=sgn))

    def start_hop(s, n, at):
        if s == 0:
            @pl.when(c == 0)
            def _():
                T[n, stage(0), :] = tokv[:, pl.ds(at, CW)]

            @pl.when(c == 1)
            def _():
                hop(0, n, at).start()

            return
        if s == 1:
            pl.when(c == 1)(lambda: hop(0, n, at).wait())
        else:
            hop(s - 1, n, at).wait()
        hop(s, n, at).start()

    def meta_copy(s):
        return remote(mine, metas.at[s], m_send.at[s], m_recv.at[s], dev(dz=sgn * (s + c)))

    def ring_slots():
        @pl.when(c == 1)
        def _():
            meta_copy(0).wait()

        for s in range(1, 4):
            meta_copy(s).wait()
        for g in range(2):
            for s2 in range(2):
                rows = []
                for yy in range(NY):
                    key = p_iota + ((z * NY + yy) * CAP).astype(F32)
                    pick = sum((metas[3 - g if s2 else g, i:i + 1, :] == key).astype(F32) for i in range(TOPK))
                    rows += [empty, pick] if s2 else [pick, empty]
                SR[g, :, s2 * TOK:(s2 + 1) * TOK] = jnp.concatenate(rows, axis=0).astype(BF16)

    def y_rows(k):
        return pl.ds(pl.multiple_of(k * YR, 16), YR)

    def y_copy(dy, g, n, u, r):
        there = lax.rem(y + dy, NY)
        return remote(GR.at[g, n, y_rows(there)], XA.at[r, u, y_rows(y)], y_send.at[dy - 1, g, n], y_recv.at[dy - 1, g, n],
                      dev(dy=dy))

    def ring_rows(g, n, u, r):
        pair = pl.ds(pl.multiple_of(g * 2 * TOK, 2 * TOK), 2 * TOK)
        GR[g, n] = jnp.dot(SR[g], T[n, pair, :], preferred_element_type=F32).astype(BF16)
        for dy in range(1, NY):
            y_copy(dy, g, n, u, r).start()
        XA[r, u, y_rows(y), :] = GR[g, n, y_rows(y), :]

    def x_copy(i, u):
        if i < 2:
            return remote(XA.at[x, u], XA.at[x, u], x_send.at[i, u], x_recv.at[i, u], dev(dx=1 - 2 * i))
        away = lax.rem(x + (3 if i == 2 else 1), NX)
        part = pl.ds(0, HALF) if i == 2 else pl.ds(HALF, HALF)
        return remote(XA.at[away, u, part], XA.at[away, u, part], x_send.at[i, u], x_recv.at[i, u], dev(dx=1 if i == 2 else -1))

    right, left, anti = lax.rem(x + 1, NX), lax.rem(x + 3, NX), lax.rem(x + 2, NX)
    lo, hi = pl.ds(0, HALF), pl.ds(HALF, HALF)

    def rx_copy(i, u):
        src, dst, dx = [
            (PX.at[u, anti, lo], RA.at[0, u], 1),
            (PX.at[u, anti, hi], RA.at[1, u], -1),
            (PX.at[u, right, hi], FX.at[0, u, hi], 1),
            (PX.at[u, left, lo], FX.at[1, u, lo], -1),
            (PX.at[u, right, lo], FX.at[0, u, lo], 1),
            (PX.at[u, left, hi], FX.at[1, u, hi], -1),
        ][i]
        return remote(src, dst, rx_send.at[i, u], rx_recv.at[i, u], dev(dx=dx))

    def piece(h, j):
        return lax.div(2 * j + h, NPIECE), lax.rem(2 * j + h, NPIECE)

    def out_copy(h, j):
        place = piece(h, j)[1]
        return remote(ZO.at[j, pl.ds(h * TOK, TOK)], O.at[place], o_send.at[h, j], o_recv.at[place], sib)

    w_copies = [
        remote(gate, wgu.at[c], w_send.at[0], w_recv.at[0], sib),
        remote(up, wgu.at[2 + c], w_send.at[1], w_recv.at[1], sib),
        remote(down, wd.at[own_rows], w_send.at[2], w_recv.at[2], sib),
    ]

    def send_rows(u):
        g, j = parts(u)
        at = col(x, j)
        both = jnp.concatenate([tokv[:, pl.ds(at, HW)], tokv[:, pl.ds(pl.multiple_of(at + HW, HW), HW)]], axis=0)
        rows = pl.ds(pl.multiple_of(g * SENT, SENT), SENT)
        GS[u] = jnp.dot(S[rows, :], both, preferred_element_type=F32).astype(BF16)
        scatter(GS, PK, a_send, a_recv, u, 1)

    @pl.when(c == 0)
    def _():
        pl.semaphore_wait(bar, 4 + 27)

    @pl.when(c == 1)
    def _():
        pl.semaphore_wait(bar, 4 + 28)

    @pl.when(c == 0)
    def _():
        metas[0] = mine[...]

    @pl.when(c == 1)
    def _():
        meta_copy(0).start()

    for s in range(1, 4):
        meta_copy(s).start()
    tok_copy.wait()
    send_rows(0)
    send_rows(1)

    @pl.loop(0, NRA)
    def _(n):
        start_hop(0, n, col(x, NK + n))

    def step(t, carry):
        def unit(lag, f):
            u = t - lag

            @pl.when(jnp.logical_and(u >= 0, u < NU))
            def _():
                f(u)

        @pl.when(jnp.logical_and(t < NU - 2, lax.rem(t + 2, NJ) < NK))
        def _():
            send_rows(t + 2)

        for s, at_a, at_d in RING:
            if s:
                @pl.when(t == at_a)
                def _():
                    @pl.loop(0, NRA)
                    def _(n):
                        start_hop(s, n, col(x, NK + n))

            @pl.when(t == at_d)
            def _():
                @pl.loop(NRA, NR)
                def _(n):
                    start_hop(s, n, col(lax.rem(n - NRA, NX), NA + lax.div(n - NRA, NX)))

        @pl.when(t == NK - 1)
        def _():
            ring_slots()

        def pick_gathered(u):
            g, j = parts(u)

            @pl.when(jnp.logical_and(j >= NK, j < NA))
            def _():
                n = j - NK
                pl.when(g == 0)(lambda: hop(3, n, 0).wait())
                ring_rows(g, n, u, x)

        unit(0, pick_gathered)

        def pick_direct(u):
            g, j = parts(u)

            @pl.when(j >= NA)
            def _():
                @pl.loop(0, NX)
                def _(r):
                    n = NRA + (j - NA) * NX + r
                    pl.when(g == 0)(lambda: hop(3, n, 0).wait())
                    ring_rows(g, n, u, r)

        unit(LD, pick_direct)

        @pl.when(t == 0)
        def _():
            for cp in w_copies:
                cp.start()
            acc[...] = jnp.zeros_like(acc)
            pick_slots(1)

        def forward(u):
            x_copy(0, u).wait()
            x_copy(2, u).start()
            x_copy(1, u).wait()
            x_copy(3, u).start()

        def gathered(f):
            return lambda u: pl.when(lax.rem(u, NJ) < NA)(lambda: f(u))


        def send_x(u):
            g, j = parts(u)

            @pl.when(j < NK)
            def _():
                all_arrived(PK, a_recv, u)
                a = PK[u].astype(F32).reshape(NB, BR, HW)
                XA[x, u] = jnp.concatenate([a[:, :CAP].reshape(ROWS, HW), a[:, CAP:].reshape(ROWS, HW)], axis=1).astype(BF16)

            @pl.when(j >= NK)
            def _():
                for dy in range(1, NY):
                    y_copy(dy, g, j - NK, u, x).wait()

            x_copy(0, u).start()
            x_copy(1, u).start()

        unit(LX, gathered(send_x))
        unit(LF, gathered(forward))

        def add_x(u):
            rx_copy(0, u).wait()
            PX[u, right, lo, :] = (PX[u, right, lo, :].astype(F32) + RA[0, u].astype(F32)).astype(BF16)
            rx_copy(4, u).start()
            rx_copy(1, u).wait()
            PX[u, left, hi, :] = (PX[u, left, hi, :].astype(F32) + RA[1, u].astype(F32)).astype(BF16)
            rx_copy(5, u).start()

        unit(LA, add_x)

        @pl.when(jnp.logical_or(t == LP, t == LP + NJ))
        def _():
            g = lax.div(t - LP, NJ)
            for i in range(2):
                v = acc[g, i]
                H[g, :, i * 256:(i + 1) * 256] = (v / (1.0 + jnp.exp(-v)) * acc[g, 2 + i]).astype(BF16)

        @pl.when(t == LP)
        def _():
            local[2].wait()
            w_copies[2].wait()

        def down_part(u):
            g, j = parts(u)

            @pl.loop(0, NX)
            def _(i):
                r = lax.rem(x + 2 + i, NX)
                PX[u, r] = jnp.dot(H[g], wd[:, pl.ds(col(r, j), CW)], preferred_element_type=F32).astype(BF16)

            for i in range(4):
                rx_copy(i, u).start()

        unit(LP, down_part)

        def sum_x(u):
            for i in range(2, 6):
                rx_copy(i, u).wait()
            a = PX[u, x].astype(F32) + FX[0, u].astype(F32) + FX[1, u].astype(F32)
            a = jnp.concatenate([a[:, :HW].reshape(NB, CAP, HW), a[:, HW:].reshape(NB, CAP, HW)], axis=1)
            GB[u] = a.reshape(SENT, HW).astype(BF16)
            scatter(GB, Q, b_send, b_recv, u, -1)

        unit(LS, sum_x)

        @pl.when(t == 1)
        def _():
            weigh_slots(0)

        @pl.when(t == 2)
        def _():
            weigh_slots(1)

        @pl.when(t == LM)
        def _():
            for cp in local[:2] + w_copies[:2]:
                cp.wait()

        def gate_up(u):
            g, j = parts(u)

            @pl.when(j < NA)
            def _():
                x_copy(2, u).wait()
                x_copy(3, u).wait()

            @pl.when(j >= NA)
            def _():
                @pl.loop(0, NX)
                def _(r):
                    for dy in range(1, NY):
                        y_copy(dy, g, NRA + (j - NA) * NX + r, u, r).wait()

            @pl.loop(0, 4)
            def _(i):
                acc[g, i] += sum(jnp.dot(XA[r, u], wgu[i, pl.ds(col(r, j), CW), :], preferred_element_type=F32)
                                 for r in range(NX))

        unit(LM, gate_up)

        def combine(u):
            g, j = parts(u)
            all_arrived(Q, b_recv, u)
            cols = pl.ds(pl.multiple_of(g * SENT, SENT), SENT)
            part = jnp.dot(WW[:, cols], Q[u], preferred_element_type=F32)

            @pl.when(g == 0)
            def _():
                ZF[j] = part

            @pl.when(g == 1)
            def _():
                ZF[j] += part
                for h in range(2):
                    @pl.when(piece(h, j)[0] != c)
                    def _():
                        ZO[j, h * TOK:(h + 1) * TOK, :] = ZF[j, h * TOK:(h + 1) * TOK, :].astype(BF16)
                        out_copy(h, j).start()

        unit(LC, combine)

        def finish(u):
            j = u - NJ

            @pl.when(j >= 0)
            def _():
                for h in range(2):
                    core, place = piece(h, j)

                    @pl.when(core == c)
                    def _():
                        out_copy(h, j).wait_recv()
                        at = pl.ds(pl.multiple_of(place * HW, HW), HW)
                        out_ref[:, at] = (ZF[j, h * TOK:(h + 1) * TOK, :] + O[place].astype(F32)).astype(BF16)

                    @pl.when(core != c)
                    def _():
                        out_copy(h, j).wait_send()

        unit(LO, finish)
        unit(LX + 2, lambda u: pl.when(lax.rem(u, NJ) < NK)(lambda: all_left(GS, a_send, u)))
        unit(LO, lambda u: all_left(GB, b_send, u))
        return carry

    lax.fori_loop(0, NU + LO, step, 0)


def per_device(tokens, expert_ids, route_score, gate_weight, up_weight, down_weight):
    vm, dma = pltpu.VMEM, pltpu.SemaphoreType.DMA
    hbm, here = pl.BlockSpec(memory_space=pl.ANY), pl.BlockSpec(memory_space=pltpu.VMEM)
    return pl.pallas_call(
        kernel,
        out_shape=jax.ShapeDtypeStruct((TOK, NPIECE * HW), BF16),
        in_specs=[here, here, hbm, hbm, hbm, hbm],
        out_specs=here,
        scratch_shapes=[
            vm((4, D, 256), BF16), vm((512, D), BF16), vm((TOK, D), BF16),
            vm((NU, SENT, HW), BF16), vm((NU, SENT, HW), BF16),
            vm((NX, NU, ROWS, CW), BF16),
            vm((2, 4, ROWS, 256), F32), vm((2, ROWS, 512), BF16),
            vm((2 * SENT, 2 * TOK), BF16), vm((2 * TOK, 2 * SENT), BF16),
            vm((NU, NX, ROWS, CW), BF16),
            vm((2, NU, HALF, CW), BF16), vm((2, NU, ROWS, CW), BF16),
            vm((NU, SENT, HW), BF16), vm((NU, SENT, HW), BF16),
            vm((NJ, 2 * TOK, HW), F32), vm((NJ, 2 * TOK, HW), BF16),
            vm((NPIECE, TOK, HW), BF16),
            vm((8, TOK), F32), vm((4, 8, TOK), F32),
            vm((NR, 4 * TOK, CW), BF16), vm((2, ROWS, 2 * TOK), BF16), vm((2, NR, ROWS, CW), BF16),
            dma((4,)), dma((3,)), dma((3,)), dma((NU,)), dma((NU,)), dma((4, NU)), dma((4, NU)),
            dma((6, NU)), dma((6, NU)), dma((NU,)), dma((NU,)), dma((2, NJ)), dma((NPIECE,)),
            dma((4,)), dma((4,)), dma((4, NR)), dma((4, NR)), dma((3, 2, NR)), dma((3, 2, NR)),
        ],
        compiler_params=pltpu.CompilerParams(collective_id=0, has_side_effects=True, vmem_limit_bytes=62 * 2**20),
        name="moe",
    )(expert_ids.T, route_score.T, tokens, gate_weight[0], up_weight[0], down_weight[0])


def solution(mesh):
    placed = (
        P("ep", None),
        P("ep", None),
        P("ep", None),
        P("ep", None, "pp"),
        P("ep", None, "pp"),
        P("ep", "pp", None),
    )
    return jax.shard_map(
        per_device, mesh=mesh, in_specs=placed, out_specs=P("ep", "pp"), check_vma=False
    )
```

```python
import jax
import jax.numpy as jnp
from jax import lax
from jax.experimental import pallas as pl
from jax.experimental.pallas import tpu as pltpu
from jax.sharding import PartitionSpec as P

MESH = pl.DeviceIdType.MESH
F32, BF16 = jnp.float32, jnp.bfloat16
D, REGION, CW, HW = 7168, 1792, 256, 128
TOK, CAP, NE, TOPK = 128, 24, 32, 4
NX, NZ, NY = 4, 8, 4
NB = 8
BR = 2 * CAP
SENT = NB * BR
ROWS = NB * CAP
HALF = ROWS // 2
NJ = REGION // CW
NU = 2 * NJ
NK, NA = 6, 6
NRA = NA - NK
NR = NRA + NX * (NJ - NA)
YR = 2 * CAP
PLACE = (0, 2, 3, 1)
NPIECE = 7
LX, LF, LM = 1, 3, 6
LP = NJ + LM
LA, LS, LC, LO = LP + 2, LP + 4, LP + 6, LP + 7
LD = 2
RING = ((0, -1, 0), (1, -1, 2), (2, -1, 4), (3, -1, 6))


def kernel(ids_ref, score_ref, tok, gate, up, down, out_ref, wgu, wd, tokv, GS, PK, XA, acc, H, S, WW, PX, RA, FX, GB, Q, ZF, ZO, O,
           mine, metas, T, SR, GR,
           l_sem, w_send, w_recv, a_send, a_recv, x_send, x_recv, rx_send, rx_recv, b_send, b_recv, o_send, o_recv,
           m_send, m_recv, z_send, z_recv, y_send, y_recv):
    pp, ep = lax.axis_index("pp"), lax.axis_index("ep")
    x, c, z, y = lax.div(pp, 2), lax.rem(pp, 2), lax.div(ep, NY), lax.rem(ep, NY)
    sgn = 2 * c - 1

    def dev(dx=0, dz=0, dy=0):
        return (lax.rem(x + dx + NX, NX) * 2 + c, lax.rem(z + dz + NZ, NZ) * NY + lax.rem(y + dy, NY))

    def remote(src, dst, ss, rs, device):
        return pltpu.make_async_remote_copy(src_ref=src, dst_ref=dst, send_sem=ss, recv_sem=rs, device_id=device,
                                            device_id_type=MESH)

    sib = (x * 2 + 1 - c, ep)
    bar = pltpu.get_barrier_semaphore()

    def greet(device):
        pl.semaphore_signal(bar, inc=1, device_id=device, device_id_type=MESH)

    for dx in (1, 2, 3):
        greet(dev(dx=dx))
    greet(sib)
    for dy in range(NY):
        for dz in (1, 2, 3, 5, 6, 7):
            greet(dev(dz=dz, dy=dy))

    @pl.when(c == 0)
    def _():
        for dy in range(1, NY):
            greet(dev(dy=dy))

    @pl.when(c == 1)
    def _():
        for dy in range(NY):
            greet(dev(dz=4, dy=dy))

    own_rows = pl.ds(pl.multiple_of(c * 256, 256), 256)
    tok_copy = pltpu.make_async_copy(tok, tokv, l_sem.at[3])
    local = [
        pltpu.make_async_copy(gate, wgu.at[c], l_sem.at[0]),
        pltpu.make_async_copy(up, wgu.at[2 + c], l_sem.at[1]),
        pltpu.make_async_copy(down, wd.at[own_rows], l_sem.at[2]),
    ]
    for cp in [tok_copy] + local:
        cp.start()

    ids, score = ids_ref[...].astype(F32), score_ref[...]
    e_iota = lax.broadcasted_iota(jnp.int32, (NE, TOK), 0).astype(F32)
    hot = [(e_iota == ids[k:k + 1, :]).astype(F32) for k in range(TOPK)]
    count = hot[0] + hot[1] + hot[2] + hot[3]
    before = (lax.broadcasted_iota(jnp.int32, (TOK, TOK), 0) < lax.broadcasted_iota(jnp.int32, (TOK, TOK), 1)).astype(F32)
    earlier = jnp.dot(count.astype(BF16), before.astype(BF16), preferred_element_type=F32)
    target = ids * CAP + jnp.concatenate([jnp.sum(h * earlier, axis=0, keepdims=True) for h in hot], axis=0)
    weight = score / jnp.sum(score, axis=0, keepdims=True)

    p_iota = lax.broadcasted_iota(jnp.int32, (CAP, TOK), 0).astype(F32)
    empty = jnp.zeros((CAP, TOK), F32)

    def slot_matches(g, k):
        expert = lax.rem(z + sgn * ((g if k % 2 == 0 else 3 - g) + c) + NZ, NZ) * NY + k // 2
        key = p_iota + (expert * CAP).astype(F32)
        return [(target[i:i + 1, :] == key).astype(F32) for i in range(TOPK)]

    def halves(a):
        return jnp.concatenate([jnp.concatenate([a, empty], axis=1), jnp.concatenate([empty, a], axis=1)], axis=0)

    def pick_slots(g):
        for k in range(NB):
            eq = slot_matches(g, k)
            at = g * SENT + k * BR
            S[at:at + BR, :] = halves(eq[0] + eq[1] + eq[2] + eq[3]).astype(BF16)

    def weigh_slots(g):
        rows = []
        for k in range(NB):
            eq = slot_matches(g, k)
            rows.append(halves(sum(eq[i] * weight[i:i + 1, :] for i in range(TOPK))))
        WW[:, g * SENT:(g + 1) * SENT] = jnp.concatenate(rows, axis=0).T.astype(BF16)

    pick_slots(0)
    mine[0:4, :] = target
    mine[4:8, :] = weight

    def parts(u):
        return lax.div(u, NJ), lax.rem(u, NJ)

    def col(r, j):
        return pl.multiple_of(REGION * r + CW * j, CW)

    def block(k):
        return pl.ds(pl.multiple_of(k * BR, 16), BR)

    def scatter(src, dst, ss, rs, u, way):
        g = lax.div(u, NJ)
        whole = jnp.logical_or(c == 1, g == 1)
        for s2 in (1, 0):
            dz = way * sgn * ((3 - g if s2 else g) + c)
            for dy in range(NY):
                cp = remote(src.at[u, block(lax.rem(y + dy, NY) * 2 + s2)], dst.at[u, block(y * 2 + s2)], ss.at[u], rs.at[u],
                            dev(dz=dz, dy=dy))
                if s2 or dy:
                    cp.start()
                else:
                    pl.when(whole)(cp.start)

        @pl.when(jnp.logical_not(whole))
        def _():
            pltpu.make_async_copy(src.at[u, block(y * 2)], dst.at[u, block(y * 2)], rs.at[u]).start()

    def all_arrived(dst, rs, u):
        remote(dst.at[u], dst.at[u], rs.at[u], rs.at[u], sib).wait_recv()

    def all_left(src, ss, u):
        whole = jnp.logical_or(c == 1, lax.div(u, NJ) == 1)

        @pl.when(whole)
        def _():
            remote(src.at[u], src.at[u], ss.at[u], ss.at[u], sib).wait_send()

        @pl.when(jnp.logical_not(whole))
        def _():
            most = src.at[u, pl.ds(0, SENT - BR)]
            remote(most, most, ss.at[u], ss.at[u], sib).wait_send()

    def stage(s):
        return pl.ds(PLACE[s] * TOK, TOK)

    def hop(s, n, at):
        src = tokv.at[:, pl.ds(at, CW)] if s == 0 else T.at[n, stage(s - 1)]
        return remote(src, T.at[n, stage(s)], z_send.at[s, n], z_recv.at[s, n], dev(dz=sgn))

    def start_hop(s, n, at):
        if s == 0:
            @pl.when(c == 0)
            def _():
                T[n, stage(0), :] = tokv[:, pl.ds(at, CW)]

            @pl.when(c == 1)
            def _():
                hop(0, n, at).start()

            return
        if s == 1:
            pl.when(c == 1)(lambda: hop(0, n, at).wait())
        else:
            hop(s - 1, n, at).wait()
        hop(s, n, at).start()

    def meta_copy(s):
        return remote(mine, metas.at[s], m_send.at[s], m_recv.at[s], dev(dz=sgn * (s + c)))

    def ring_slots():
        @pl.when(c == 1)
        def _():
            meta_copy(0).wait()

        for s in range(1, 4):
            meta_copy(s).wait()
        for g in range(2):
            for s2 in range(2):
                rows = []
                for yy in range(NY):
                    key = p_iota + ((z * NY + yy) * CAP).astype(F32)
                    pick = sum((metas[3 - g if s2 else g, i:i + 1, :] == key).astype(F32) for i in range(TOPK))
                    rows += [empty, pick] if s2 else [pick, empty]
                SR[g, :, s2 * TOK:(s2 + 1) * TOK] = jnp.concatenate(rows, axis=0).astype(BF16)

    def y_rows(k):
        return pl.ds(pl.multiple_of(k * YR, 16), YR)

    def y_copy(dy, g, n, u, r):
        there = lax.rem(y + dy, NY)
        return remote(GR.at[g, n, y_rows(there)], XA.at[r, u, y_rows(y)], y_send.at[dy - 1, g, n], y_recv.at[dy - 1, g, n],
                      dev(dy=dy))

    def ring_rows(g, n, u, r):
        pair = pl.ds(pl.multiple_of(g * 2 * TOK, 2 * TOK), 2 * TOK)
        GR[g, n] = jnp.dot(SR[g], T[n, pair, :], preferred_element_type=F32).astype(BF16)
        for dy in range(1, NY):
            y_copy(dy, g, n, u, r).start()
        XA[r, u, y_rows(y), :] = GR[g, n, y_rows(y), :]

    def x_copy(i, u):
        if i < 2:
            return remote(XA.at[x, u], XA.at[x, u], x_send.at[i, u], x_recv.at[i, u], dev(dx=1 - 2 * i))
        away = lax.rem(x + (3 if i == 2 else 1), NX)
        part = pl.ds(0, HALF) if i == 2 else pl.ds(HALF, HALF)
        return remote(XA.at[away, u, part], XA.at[away, u, part], x_send.at[i, u], x_recv.at[i, u], dev(dx=1 if i == 2 else -1))

    right, left, anti = lax.rem(x + 1, NX), lax.rem(x + 3, NX), lax.rem(x + 2, NX)
    lo, hi = pl.ds(0, HALF), pl.ds(HALF, HALF)

    def rx_copy(i, u):
        src, dst, dx = [
            (PX.at[u, anti, lo], RA.at[0, u], 1),
            (PX.at[u, anti, hi], RA.at[1, u], -1),
            (PX.at[u, right, hi], FX.at[0, u, hi], 1),
            (PX.at[u, left, lo], FX.at[1, u, lo], -1),
            (PX.at[u, right, lo], FX.at[0, u, lo], 1),
            (PX.at[u, left, hi], FX.at[1, u, hi], -1),
        ][i]
        return remote(src, dst, rx_send.at[i, u], rx_recv.at[i, u], dev(dx=dx))

    def piece(h, j):
        return lax.div(2 * j + h, NPIECE), lax.rem(2 * j + h, NPIECE)

    def out_copy(h, j):
        place = piece(h, j)[1]
        return remote(ZO.at[j, pl.ds(h * TOK, TOK)], O.at[place], o_send.at[h, j], o_recv.at[place], sib)

    w_copies = [
        remote(gate, wgu.at[c], w_send.at[0], w_recv.at[0], sib),
        remote(up, wgu.at[2 + c], w_send.at[1], w_recv.at[1], sib),
        remote(down, wd.at[own_rows], w_send.at[2], w_recv.at[2], sib),
    ]

    def send_rows(u):
        g, j = parts(u)
        at = col(x, j)
        both = jnp.concatenate([tokv[:, pl.ds(at, HW)], tokv[:, pl.ds(pl.multiple_of(at + HW, HW), HW)]], axis=0)
        rows = pl.ds(pl.multiple_of(g * SENT, SENT), SENT)
        GS[u] = jnp.dot(S[rows, :], both, preferred_element_type=F32).astype(BF16)
        scatter(GS, PK, a_send, a_recv, u, 1)

    @pl.when(c == 0)
    def _():
        pl.semaphore_wait(bar, 4 + 27)

    @pl.when(c == 1)
    def _():
        pl.semaphore_wait(bar, 4 + 28)

    @pl.when(c == 0)
    def _():
        metas[0] = mine[...]

    @pl.when(c == 1)
    def _():
        meta_copy(0).start()

    for s in range(1, 4):
        meta_copy(s).start()
    tok_copy.wait()
    send_rows(0)
    send_rows(1)

    @pl.loop(0, NRA)
    def _(n):
        start_hop(0, n, col(x, NK + n))

    def step(t, carry):
        def unit(lag, f):
            u = t - lag

            @pl.when(jnp.logical_and(u >= 0, u < NU))
            def _():
                f(u)

        @pl.when(jnp.logical_and(t < NU - 2, lax.rem(t + 2, NJ) < NK))
        def _():
            send_rows(t + 2)

        for s, at_a, at_d in RING:
            if s:
                @pl.when(t == at_a)
                def _():
                    @pl.loop(0, NRA)
                    def _(n):
                        start_hop(s, n, col(x, NK + n))

            @pl.when(t == at_d)
            def _():
                @pl.loop(NRA, NR)
                def _(n):
                    start_hop(s, n, col(lax.rem(n - NRA, NX), NA + lax.div(n - NRA, NX)))

        @pl.when(t == NK - 1)
        def _():
            ring_slots()

        def pick_gathered(u):
            g, j = parts(u)

            @pl.when(jnp.logical_and(j >= NK, j < NA))
            def _():
                n = j - NK
                pl.when(g == 0)(lambda: hop(3, n, 0).wait())
                ring_rows(g, n, u, x)

        unit(0, pick_gathered)

        def pick_direct(u):
            g, j = parts(u)

            @pl.when(j >= NA)
            def _():
                @pl.loop(0, NX)
                def _(r):
                    n = NRA + (j - NA) * NX + r
                    pl.when(g == 0)(lambda: hop(3, n, 0).wait())
                    ring_rows(g, n, u, r)

        unit(LD, pick_direct)

        @pl.when(t == 0)
        def _():
            for cp in w_copies:
                cp.start()
            acc[...] = jnp.zeros_like(acc)
            pick_slots(1)

        def forward(u):
            x_copy(0, u).wait()
            x_copy(2, u).start()
            x_copy(1, u).wait()
            x_copy(3, u).start()

        def gathered(f):
            return lambda u: pl.when(lax.rem(u, NJ) < NA)(lambda: f(u))


        def send_x(u):
            g, j = parts(u)

            @pl.when(j < NK)
            def _():
                all_arrived(PK, a_recv, u)
                a = PK[u].astype(F32).reshape(NB, BR, HW)
                XA[x, u] = jnp.concatenate([a[:, :CAP].reshape(ROWS, HW), a[:, CAP:].reshape(ROWS, HW)], axis=1).astype(BF16)

            @pl.when(j >= NK)
            def _():
                for dy in range(1, NY):
                    y_copy(dy, g, j - NK, u, x).wait()

            x_copy(0, u).start()
            x_copy(1, u).start()

        unit(LX, gathered(send_x))
        unit(LF, gathered(forward))

        def add_x(u):
            rx_copy(0, u).wait()
            PX[u, right, lo, :] = (PX[u, right, lo, :].astype(F32) + RA[0, u].astype(F32)).astype(BF16)
            rx_copy(4, u).start()
            rx_copy(1, u).wait()
            PX[u, left, hi, :] = (PX[u, left, hi, :].astype(F32) + RA[1, u].astype(F32)).astype(BF16)
            rx_copy(5, u).start()

        unit(LA, add_x)

        @pl.when(jnp.logical_or(t == LP, t == LP + NJ))
        def _():
            g = lax.div(t - LP, NJ)
            for i in range(2):
                v = acc[g, i]
                H[g, :, i * 256:(i + 1) * 256] = (v / (1.0 + jnp.exp(-v)) * acc[g, 2 + i]).astype(BF16)

        @pl.when(t == LP)
        def _():
            local[2].wait()
            w_copies[2].wait()

        def down_part(u):
            g, j = parts(u)

            @pl.loop(0, NX)
            def _(i):
                r = lax.rem(x + 2 + i, NX)
                PX[u, r] = jnp.dot(H[g], wd[:, pl.ds(col(r, j), CW)], preferred_element_type=F32).astype(BF16)

                @pl.when(i == 0)
                def _():
                    rx_copy(0, u).start()
                    rx_copy(1, u).start()

                pl.when(i == 1)(lambda: rx_copy(3, u).start())
                pl.when(i == 3)(lambda: rx_copy(2, u).start())

        unit(LP, down_part)

        def sum_x(u):
            for i in range(2, 6):
                rx_copy(i, u).wait()
            a = PX[u, x].astype(F32) + FX[0, u].astype(F32) + FX[1, u].astype(F32)
            a = jnp.concatenate([a[:, :HW].reshape(NB, CAP, HW), a[:, HW:].reshape(NB, CAP, HW)], axis=1)
            GB[u] = a.reshape(SENT, HW).astype(BF16)
            scatter(GB, Q, b_send, b_recv, u, -1)

        unit(LS, sum_x)

        @pl.when(t == 1)
        def _():
            weigh_slots(0)

        @pl.when(t == 2)
        def _():
            weigh_slots(1)

        @pl.when(t == LM)
        def _():
            for cp in local[:2] + w_copies[:2]:
                cp.wait()

        def gate_up(u):
            g, j = parts(u)

            @pl.when(j < NA)
            def _():
                x_copy(2, u).wait()
                x_copy(3, u).wait()

            @pl.when(j >= NA)
            def _():
                @pl.loop(0, NX)
                def _(r):
                    for dy in range(1, NY):
                        y_copy(dy, g, NRA + (j - NA) * NX + r, u, r).wait()

            @pl.loop(0, 4)
            def _(i):
                acc[g, i] += sum(jnp.dot(XA[r, u], wgu[i, pl.ds(col(r, j), CW), :], preferred_element_type=F32)
                                 for r in range(NX))

        unit(LM, gate_up)

        def combine(u):
            g, j = parts(u)
            all_arrived(Q, b_recv, u)
            cols = pl.ds(pl.multiple_of(g * SENT, SENT), SENT)
            part = jnp.dot(WW[:, cols], Q[u], preferred_element_type=F32)

            @pl.when(g == 0)
            def _():
                ZF[j] = part

            @pl.when(g == 1)
            def _():
                ZF[j] += part
                for h in range(2):
                    @pl.when(piece(h, j)[0] != c)
                    def _():
                        ZO[j, h * TOK:(h + 1) * TOK, :] = ZF[j, h * TOK:(h + 1) * TOK, :].astype(BF16)
                        out_copy(h, j).start()

        unit(LC, combine)

        def finish(u):
            j = u - NJ

            @pl.when(j >= 0)
            def _():
                for h in range(2):
                    core, place = piece(h, j)

                    @pl.when(core == c)
                    def _():
                        out_copy(h, j).wait_recv()
                        at = pl.ds(pl.multiple_of(place * HW, HW), HW)
                        out_ref[:, at] = (ZF[j, h * TOK:(h + 1) * TOK, :] + O[place].astype(F32)).astype(BF16)

                    @pl.when(core != c)
                    def _():
                        out_copy(h, j).wait_send()

        unit(LO, finish)
        unit(LX + 2, lambda u: pl.when(lax.rem(u, NJ) < NK)(lambda: all_left(GS, a_send, u)))
        unit(LO, lambda u: all_left(GB, b_send, u))
        return carry

    lax.fori_loop(0, NU + LO, step, 0)


def per_device(tokens, expert_ids, route_score, gate_weight, up_weight, down_weight):
    vm, dma = pltpu.VMEM, pltpu.SemaphoreType.DMA
    hbm, here = pl.BlockSpec(memory_space=pl.ANY), pl.BlockSpec(memory_space=pltpu.VMEM)
    return pl.pallas_call(
        kernel,
        out_shape=jax.ShapeDtypeStruct((TOK, NPIECE * HW), BF16),
        in_specs=[here, here, hbm, hbm, hbm, hbm],
        out_specs=here,
        scratch_shapes=[
            vm((4, D, 256), BF16), vm((512, D), BF16), vm((TOK, D), BF16),
            vm((NU, SENT, HW), BF16), vm((NU, SENT, HW), BF16),
            vm((NX, NU, ROWS, CW), BF16),
            vm((2, 4, ROWS, 256), F32), vm((2, ROWS, 512), BF16),
            vm((2 * SENT, 2 * TOK), BF16), vm((2 * TOK, 2 * SENT), BF16),
            vm((NU, NX, ROWS, CW), BF16),
            vm((2, NU, HALF, CW), BF16), vm((2, NU, ROWS, CW), BF16),
            vm((NU, SENT, HW), BF16), vm((NU, SENT, HW), BF16),
            vm((NJ, 2 * TOK, HW), F32), vm((NJ, 2 * TOK, HW), BF16),
            vm((NPIECE, TOK, HW), BF16),
            vm((8, TOK), F32), vm((4, 8, TOK), F32),
            vm((NR, 4 * TOK, CW), BF16), vm((2, ROWS, 2 * TOK), BF16), vm((2, NR, ROWS, CW), BF16),
            dma((4,)), dma((3,)), dma((3,)), dma((NU,)), dma((NU,)), dma((4, NU)), dma((4, NU)),
            dma((6, NU)), dma((6, NU)), dma((NU,)), dma((NU,)), dma((2, NJ)), dma((NPIECE,)),
            dma((4,)), dma((4,)), dma((4, NR)), dma((4, NR)), dma((3, 2, NR)), dma((3, 2, NR)),
        ],
        compiler_params=pltpu.CompilerParams(collective_id=0, has_side_effects=True, vmem_limit_bytes=62 * 2**20),
        name="moe",
    )(expert_ids.T, route_score.T, tokens, gate_weight[0], up_weight[0], down_weight[0])


def solution(mesh):
    placed = (
        P("ep", None),
        P("ep", None),
        P("ep", None),
        P("ep", None, "pp"),
        P("ep", None, "pp"),
        P("ep", "pp", None),
    )
    return jax.shard_map(
        per_device, mesh=mesh, in_specs=placed, out_specs=P("ep", "pp"), check_vma=False
    )
```
